32 devices in a mesh: seq: 2 (over y), col: 4 (over z), tp: 4 (over x, core).
Axes of the slice: x: 2, y: 2, z: 4, core: 2. Of those that a mesh axis runs over, the one named last changes fastest.
Arguments:
- inputs: bfloat16 [4096, 8192], P(('seq', 'tp'), 'col'), may hold values from -6 to 6
- grads: bfloat16 [4096, 8192], P(('seq', 'tp'), 'col'), may hold values from -0.035888672 to 0.035888672
- h_in: bfloat16 [8192, 8192], P(None, 'col'), may hold values from -0.0625 to 0.0625
- segments: int32 [8, 512], P(('seq', 'tp')), may hold values from 0 to 3, never falling along the last dimension, each value on 1 to 256 neighbouring positions
Outputs:
- h_out: float32 [8192, 8192], P(('seq', 'tp'), 'col')
The draws below stay inside these ranges and needn't reach their ends.
Inputs may be any that keep to these rules, and one draw needn't show every extreme that they name: `segments`: within each sequence the numbers never fall; every document has 1 to 256 tokens.
All inputs are finite; a program needn't handle non-finite values.
Results may differ from the reference program's by a relative error of at most 0.005.
Values may be sent and summed in bfloat16 or wider, within the bound.
A program may use at most 128 MiB of HBM per device.

```python
import math
import jax
import jax.numpy as jnp
import numpy as np

DIN = 8192
DOUT = 8192
SEQ_LEN = 512
SEQS = 8


def level_of(key, shape, cuts, low, largest):
    gain = 1.0
    for position, parts in cuts:
        heights = jax.random.uniform(jax.random.fold_in(jax.random.fold_in(key, 6), position), (parts,), jnp.float32, low / len(cuts), largest / len(cuts))
        gain = gain * jnp.repeat(jnp.exp(heights), shape[position] // parts).reshape((-1,) + (1,) * (len(shape) - 1 - position))
    return gain


def profile(amount, total, most, lean):
    weights = [(1 << 20) // math.isqrt(rank ** lean) + 1 for rank in range(2, amount + 1)]
    rest, given = total - most - (amount - 1), [1] * (amount - 1)
    while rest > 0:
        free = [i for i in range(amount - 1) if given[i] < most]
        pool, remaining = sum([weights[i] for i in free]), rest
        for i in free:
            extra = min(most - given[i], max(1, remaining * weights[i] // pool), rest)
            given[i] = given[i] + extra
            rest = rest - extra
    return np.array([most] + given)


def uneven(own_key, amount, total, most, lean):
    if amount == 2:
        one = jax.random.randint(own_key, (), max(1, total - most), min(most, total - 1) + 1)
        return jnp.stack([one, total - one])
    tallies = jnp.asarray(profile(amount, total, most, lean), jnp.int32)
    pairs = (amount - 1) // 2
    source_of, taker = tallies[1:1 + 2 * pairs:2], tallies[2:2 + 2 * pairs:2]
    room = jnp.minimum(source_of - 1, most - taker)
    shifted = jax.random.randint(jax.random.fold_in(own_key, 1), (pairs,), 0, 1 << 20) % (room + 1)
    tallies = tallies.at[1:1 + 2 * pairs:2].set(source_of - shifted).at[2:2 + 2 * pairs:2].set(taker + shifted)
    return tallies[jax.random.permutation(jax.random.fold_in(own_key, 2), amount)]


def noise(key, dims, deviation, limit, shards=(), dtype=jnp.bfloat16):
    drawn = jax.random.normal(key, dims, jnp.float32) * deviation
    if len(shards) > 0:
        drawn = level_of(key, dims, shards, -0.22, 0.18) * drawn
    return jnp.clip(drawn, min=-limit, max=limit).astype(dtype)


def setup_inputs(seed: int = 0) -> dict:
    keys = jax.random.split(jax.random.key(seed), 5)
    return {
        "inputs": noise(keys[0], (SEQS * SEQ_LEN, DIN), 1.0, 6.0, ((0, 8), (1, 4))),
        "grads": noise(keys[1], (SEQS * SEQ_LEN, DOUT), 0.006, 0.035888672, ((0, 8), (1, 4))),
        "h_in": noise(keys[2], (DIN, DIN), DIN ** -0.5, 0.0625, ((1, 4),)),
        "segments": jax.vmap(lambda own: jnp.searchsorted(jnp.cumsum(uneven(own, 4, SEQ_LEN, SEQ_LEN // 2, 0)), jnp.arange(SEQ_LEN), side="right"))(jax.random.split(keys[3], SEQS)).reshape((SEQS, SEQ_LEN)).astype(jnp.int32),
    }


def reference(inputs, grads, h_in, segments):
    summed = jnp.zeros((DOUT, DOUT), jnp.float32)
    for sequence in range(SEQS):
        lower = sequence * SEQ_LEN
        x_rows = inputs[lower:lower + SEQ_LEN]
        d_rows = grads[lower:lower + SEQ_LEN]
        projected = jnp.dot(x_rows, h_in, preferred_element_type=jnp.float32).astype(jnp.bfloat16)
        square = jnp.dot(projected, x_rows.T, preferred_element_type=jnp.float32)
        labels = segments[sequence]
        same = labels[:, None] == labels[None, :]
        masked = jnp.where(same, square, jnp.float32(0.0)).astype(jnp.bfloat16)
        product = jnp.dot(masked, d_rows, preferred_element_type=jnp.float32).astype(jnp.bfloat16)
        summed = summed + jnp.dot(d_rows.T, product, preferred_element_type=jnp.float32)
    return summed
```

```python
import functools

import jax
import jax.numpy as jnp
from jax import lax
from jax.experimental import pallas as pl
from jax.experimental.pallas import tpu as pltpu
from jax.sharding import PartitionSpec as P

MESH = pl.DeviceIdType.MESH
MIB = 1 << 20


def gather_kernel(
    n, tps, planes, out_rows,
    x_ref, d_ref, h_ref, seg_ref, segt_ref,
    dr_ref, dc_ref, k_ref,
    xg, dg, hbuf, y, pp, pin, krow,
    x_send, x_recv, d_send, d_recv, c_send, c_recv, a_send, a_recv,
    p_send, p_recv, kz_send, kz_recv, k_send, k_recv, local, h_sem,
):
    rows, cols = x_ref.shape
    width = min(cols, out_rows)
    pieces, per_row_block = cols // width, out_rows // width
    half = planes // 2
    part = rows // n
    tile = min(cols, 256)
    c = lax.axis_index("col")
    p = lax.axis_index("seq") * tps + lax.axis_index("tp")
    parity, mate = lax.rem(p, 2), p + 1 - 2 * lax.rem(p, 2)
    pending = []

    def in_plane(index):
        return {"seq": index // tps, "tp": lax.rem(index, tps)}

    def same_parity(step):
        return 2 * lax.rem(p // 2 + step + half, half) + parity

    def send(make, condition=None):
        if condition is None:
            make().start()
        else:
            pl.when(condition)(lambda: make().start())
        pending.append((make, condition))

    def remote(src, dst, ssem, rsem, to):
        return pltpu.make_async_remote_copy(
            src_ref=src, dst_ref=dst, send_sem=ssem, recv_sem=rsem,
            device_id=to, device_id_type=MESH,
        )

    barrier = pltpu.get_barrier_semaphore()
    for step in range(1, n):
        pl.semaphore_signal(
            barrier, inc=1, device_id={"col": lax.rem(c + step, n)}, device_id_type=MESH
        )
    for step in range(1, planes):
        pl.semaphore_signal(
            barrier, inc=1, device_id=in_plane(lax.rem(p + step, planes)), device_id_type=MESH
        )
    pl.semaphore_wait(barrier, n - 1 + planes - 1)

    def pass_on(src, ring, ssem, rsem, chunk, direction, slot):
        to = c + direction
        ok = (chunk >= 0) & (chunk < n) & (to >= 0) & (to < n)

        def make():
            return remote(src(chunk), ring.at[chunk], ssem.at[slot], rsem.at[chunk], {"col": to})

        send(make, ok)

    def received(ring, ssem, rsem, chunk):
        return remote(ring.at[chunk], ring.at[chunk], ssem.at[0], rsem.at[chunk], {"col": lax.rem(c + 1, n)})

    for side in (0, 1):
        pass_on(lambda chunk: x_ref, xg, x_send, x_recv, c, 1 - 2 * side, side)
    own_x = pltpu.make_async_copy(x_ref, xg.at[c], local.at[0])
    own_x.start()

    def block(ref, index):
        return ref.at[pl.ds(index * rows, rows)]

    own_d = pltpu.make_async_copy(d_ref, block(dc_ref, p), local.at[1])
    own_d.start()
    send(lambda: remote(d_ref, block(dc_ref, p), c_send.at[0], c_recv.at[p], in_plane(mate)))
    for step in range(1, half):
        send(lambda step=step: remote(
            d_ref, block(dc_ref, p), c_send.at[step], c_recv.at[p], in_plane(same_parity(step))
        ))

    def owned(src, chunk, slot):
        for k in range(pieces):
            first = chunk * cols + k * width
            target = first // out_rows
            place = (first - target * out_rows) // width
            ok = (chunk >= 0) & (chunk < n)

            def ends():
                dst = dr_ref.at[
                    pl.ds(p * rows, rows),
                    pl.ds(pl.multiple_of(place * width, width), width),
                ]
                return src(chunk).at[:, pl.ds(k * width, width)], dst, a_recv.at[p, place]

            def make_remote(ends=ends, target=target, k=k):
                s, t, sem = ends()
                return remote(s, t, a_send.at[slot, k], sem, in_plane(target))

            def make_local(ends=ends):
                return pltpu.make_async_copy(*ends())

            send(make_remote, ok & (target != p))
            pl.when(ok & (target == p))(lambda m=make_local: m().start())

    owned(lambda chunk: d_ref, c, 0)

    def work(chunk, wait, first, forward):
        load = pltpu.make_async_copy(
            h_ref.at[pl.ds(pl.multiple_of(chunk * cols, cols), cols)], hbuf, h_sem
        )
        load.start()
        wait()
        forward()
        load.wait()

        @pl.loop(0, cols // tile)
        def _(j):
            at = pl.ds(pl.multiple_of(j * tile, tile), tile)
            term = jnp.dot(xg[chunk], hbuf[:, at], preferred_element_type=jnp.float32)
            y[:, at] = term if first else y[:, at] + term

    work(c, own_x.wait, True, lambda: None)
    for d in range(1, n):
        for side in (0, 1):
            direction = 1 - 2 * side
            chunk = c - direction * d
            ok = (chunk >= 0) & (chunk < n)
            to = c + direction
            slot = 2 * d + side

            def make(chunk=chunk, to=to, slot=slot):
                return remote(xg.at[chunk], xg.at[chunk], x_send.at[slot], x_recv.at[chunk], {"col": to})

            @pl.when(ok)
            def _():
                def forward():
                    if d < n - 1:
                        pl.when((to >= 0) & (to < n))(lambda: make().start())

                work(chunk, lambda: received(xg, x_send, x_recv, chunk).wait_recv(), False, forward)

            if d < n - 1:
                pending.append((make, ok & (to >= 0) & (to < n)))

    for side in (0, 1):
        pass_on(lambda chunk: d_ref, dg, d_send, d_recv, c, 1 - 2 * side, side)

    pp[...] = jnp.zeros_like(pp)

    @pl.loop(0, cols // tile)
    def _(j):
        at = pl.ds(pl.multiple_of(j * tile, tile), tile)
        pp[...] += lax.dot_general(
            y[:, at].astype(jnp.bfloat16), xg[c, :, at],
            (((1,), (1,)), ((), ())), preferred_element_type=jnp.float32,
        )

    def rows_of(ref, index):
        return ref.at[pl.ds(pl.multiple_of(index * part, part), part)]

    for step in range(1, n):
        to = lax.rem(c + step, n)
        send(lambda step=step, to=to: remote(
            rows_of(pp, to), pin.at[c], p_send.at[step], p_recv.at[c], {"col": to}
        ))

    def d_step(d):
        for side in (0, 1):
            direction = 1 - 2 * side
            chunk = c - direction * d
            ok = (chunk >= 0) & (chunk < n)
            pl.when(ok)(lambda: received(dg, d_send, d_recv, chunk).wait_recv())
            if d < n - 1:
                pass_on(lambda ch: dg.at[ch], dg, d_send, d_recv, chunk, direction, 2 * d + side)
            owned(lambda ch: dg.at[ch], chunk, 2 * d + side)

    def c_step():
        for step in range(1, half):
            source = same_parity(-step)
            remote(
                d_ref, block(dc_ref, source), c_send.at[0], c_recv.at[source], in_plane(mate)
            ).wait_recv()
            send(lambda step=step, source=source: remote(
                block(dc_ref, source), block(dc_ref, source),
                c_send.at[half + step], c_recv.at[source], in_plane(mate),
            ))

    def sum_step():
        total = rows_of(pp, c)[...]
        for step in range(1, n):
            source = lax.rem(c - step + n, n)
            remote(
                rows_of(pp, source), pin.at[source], p_send.at[1], p_recv.at[source],
                {"col": source},
            ).wait_recv()
            total = total + pin[source]
        same = rows_of(segt_ref, c)[...] == seg_ref[...]
        krow[...] = jnp.where(same, total, jnp.float32(0.0)).astype(jnp.bfloat16)
        dst = rows_of(k_ref.at[p], c)
        own_k = pltpu.make_async_copy(krow, dst, local.at[2])
        own_k.start()
        for step in range(1, n):
            to = lax.rem(c + step, n)
            send(lambda step=step, to=to: remote(
                krow, rows_of(k_ref.at[p], c), kz_send.at[step], kz_recv.at[c], {"col": to}
            ))
        own_k.wait()

    def square_step():
        for step in range(1, n):
            source = lax.rem(c - step + n, n)
            remote(
                krow, rows_of(k_ref.at[p], source), kz_send.at[1], kz_recv.at[source],
                {"col": source},
            ).wait_recv()
        send(lambda: remote(k_ref.at[p], k_ref.at[p], k_send.at[0], k_recv.at[p], in_plane(mate)))
        for step in range(1, half):
            send(lambda step=step: remote(
                k_ref.at[p], k_ref.at[p], k_send.at[step], k_recv.at[p],
                in_plane(same_parity(step)),
            ))

    def square_relay():
        for step in range(1, half):
            source = same_parity(-step)
            remote(
                k_ref.at[p], k_ref.at[source], k_send.at[0], k_recv.at[source], in_plane(mate)
            ).wait_recv()
            send(lambda step=step, source=source: remote(
                k_ref.at[source], k_ref.at[source],
                k_send.at[half + step], k_recv.at[source], in_plane(mate),
            ))

    c_step()
    stages = [sum_step, square_step, square_relay]
    for d in range(1, max(n, 4)):
        if stages:
            stages.pop(0)()
        if d < n:
            d_step(d)

    for step in range(half):
        other = 2 * lax.rem(p // 2 + step, half) + 1 - parity
        remote(
            d_ref, block(dc_ref, other), c_send.at[0], c_recv.at[other], in_plane(mate)
        ).wait_recv()
        remote(
            k_ref.at[p], k_ref.at[other], k_send.at[0], k_recv.at[other], in_plane(mate)
        ).wait_recv()
    for source in range(planes):
        for place in range(per_row_block):
            dst = dr_ref.at[pl.ds(source * rows, rows), pl.ds(place * width, width)]
            pltpu.make_async_copy(dst, dst, a_recv.at[source, place]).wait()
    own_d.wait()
    for make, condition in pending:
        if condition is None:
            make().wait_send()
        else:
            pl.when(condition)(lambda make=make: make().wait_send())


def product_kernel(k_ref, dc_ref, dr_ref, out_ref, turned):
    step = pl.program_id(0)
    cols = dc_ref.shape[1]
    tile = min(cols, 512)
    turned[...] = dr_ref[...].T

    @pl.when(step == 0)
    def _():
        out_ref[...] = jnp.zeros_like(out_ref)

    @pl.loop(0, cols // tile)
    def _(j):
        at = pl.ds(pl.multiple_of(j * tile, tile), tile)
        z = jnp.dot(k_ref[0], dc_ref[:, at], preferred_element_type=jnp.float32)
        out_ref[:, at] += jnp.dot(
            turned[...], z.astype(jnp.bfloat16), preferred_element_type=jnp.float32
        )


def per_device(n, seqs, tps, inputs, grads, h_in, segments):
    rows, cols = inputs.shape
    planes = seqs * tps
    out_rows = n * cols // planes
    width = min(cols, out_rows)
    part = rows // n
    dma = pltpu.SemaphoreType.DMA
    any_space = pl.BlockSpec(memory_space=pl.ANY)
    vmem = pl.BlockSpec(memory_space=pltpu.VMEM)
    owned_grads, plane_grads, squares = pl.pallas_call(
        functools.partial(gather_kernel, n, tps, planes, out_rows),
        out_shape=(
            jax.ShapeDtypeStruct((planes * rows, out_rows), jnp.bfloat16),
            jax.ShapeDtypeStruct((planes * rows, cols), jnp.bfloat16),
            jax.ShapeDtypeStruct((planes, rows, rows), jnp.bfloat16),
        ),
        in_specs=[any_space, any_space, any_space, vmem, vmem],
        out_specs=(any_space, any_space, any_space),
        scratch_shapes=[
            pltpu.VMEM((n, rows, cols), jnp.bfloat16),
            pltpu.VMEM((n, rows, cols), jnp.bfloat16),
            pltpu.VMEM((cols, cols), jnp.bfloat16),
            pltpu.VMEM((rows, cols), jnp.float32),
            pltpu.VMEM((rows, rows), jnp.float32),
            pltpu.VMEM((n, part, rows), jnp.float32),
            pltpu.VMEM((part, rows), jnp.bfloat16),
            dma((2 * n,)), dma((n,)),
            dma((2 * n,)), dma((n,)),
            dma((planes,)), dma((planes,)),
            dma((2 * n, cols // width)), dma((planes, out_rows // width)),
            dma((n,)), dma((n,)),
            dma((n,)), dma((n,)),
            dma((planes,)), dma((planes,)),
            dma((3,)), dma,
        ],
        compiler_params=pltpu.CompilerParams(
            collective_id=0, has_side_effects=True, vmem_limit_bytes=48 * MIB
        ),
    )(inputs, grads, h_in, segments, segments.reshape(rows, 1))
    return pl.pallas_call(
        product_kernel,
        grid=(planes,),
        out_shape=jax.ShapeDtypeStruct((out_rows, cols), jnp.float32),
        in_specs=[
            pl.BlockSpec((1, rows, rows), lambda s: (s, 0, 0)),
            pl.BlockSpec((rows, cols), lambda s: (s, 0)),
            pl.BlockSpec((rows, out_rows), lambda s: (s, 0)),
        ],
        out_specs=pl.BlockSpec((out_rows, cols), lambda s: (0, 0)),
        scratch_shapes=[pltpu.VMEM((out_rows, rows), jnp.bfloat16)],
        compiler_params=pltpu.CompilerParams(vmem_limit_bytes=48 * MIB),
    )(squares, plane_grads, owned_grads)


def solution(mesh):
    placed = (
        P(("seq", "tp"), "col"),
        P(("seq", "tp"), "col"),
        P(None, "col"),
        P(("seq", "tp"), None),
    )
    sizes = (mesh.shape["col"], mesh.shape["seq"], mesh.shape["tp"])
    return jax.shard_map(
        functools.partial(per_device, *sizes),
        mesh=mesh, in_specs=placed, out_specs=P(("seq", "tp"), "col"), check_vma=False,
    )
```

```python
import functools

import jax
import jax.numpy as jnp
from jax import lax
from jax.experimental import pallas as pl
from jax.experimental.pallas import tpu as pltpu
from jax.sharding import PartitionSpec as P

MESH = pl.DeviceIdType.MESH
MIB = 1 << 20


def gather_kernel(
    n, tps, planes, out_rows, slabs,
    x_ref, d_ref, h_ref, seg_ref, segt_ref,
    dr_ref, dc_ref, k_ref, z_ref,
    xg, dg, hbuf, y, pp, pin, krow, dbuf, kbuf, zbuf,
    x_send, x_recv, d_send, d_recv, c_send, c_recv, a_send, a_recv,
    p_send, p_recv, kz_send, kz_recv, k_send, k_recv, local, h_sem, z_sem,
):
    rows, cols = x_ref.shape
    width = min(cols, out_rows)
    pieces, per_row_block = cols // width, out_rows // width
    half = planes // 2
    part, slab = rows // n, rows // slabs
    tile = min(cols, 256)
    c = lax.axis_index("col")
    p = lax.axis_index("seq") * tps + lax.axis_index("tp")
    parity, mate = lax.rem(p, 2), p + 1 - 2 * lax.rem(p, 2)
    pending = []

    def in_plane(index):
        return {"seq": index // tps, "tp": lax.rem(index, tps)}

    def same_parity(step):
        return 2 * lax.rem(p // 2 + step + half, half) + parity

    def send(make, condition=None):
        if condition is None:
            make().start()
        else:
            pl.when(condition)(lambda: make().start())
        pending.append((make, condition))

    def remote(src, dst, ssem, rsem, to):
        return pltpu.make_async_remote_copy(
            src_ref=src, dst_ref=dst, send_sem=ssem, recv_sem=rsem,
            device_id=to, device_id_type=MESH,
        )

    barrier = pltpu.get_barrier_semaphore()
    for step in range(1, n):
        pl.semaphore_signal(
            barrier, inc=1, device_id={"col": lax.rem(c + step, n)}, device_id_type=MESH
        )
    for step in range(1, planes):
        pl.semaphore_signal(
            barrier, inc=1, device_id=in_plane(lax.rem(p + step, planes)), device_id_type=MESH
        )
    pl.semaphore_wait(barrier, n - 1 + planes - 1)

    for side in (0, 1):
        def make(side=side):
            return remote(x_ref, xg.at[c], x_send.at[side], x_recv.at[c], {"col": c + 1 - 2 * side})

        send(make, (c > 0) if side else (c + 1 < n))
    own_x = pltpu.make_async_copy(x_ref, xg.at[c], local.at[0])
    own_x.start()

    def block(ref, index):
        return ref.at[pl.ds(index * rows, rows)]

    own_d = pltpu.make_async_copy(d_ref, block(dc_ref, p), local.at[1])
    own_d.start()
    send(lambda: remote(d_ref, block(dc_ref, p), c_send.at[0], c_recv.at[p], in_plane(mate)))
    for step in range(1, half):
        send(lambda step=step: remote(
            d_ref, block(dc_ref, p), c_send.at[step], c_recv.at[p], in_plane(same_parity(step))
        ))

    def slab_of(ref, i):
        return ref.at[pl.ds(i * slab, slab)]

    def pass_on(src, chunk, direction, slot, i):
        to = c + direction
        ok = (chunk >= 0) & (chunk < n) & (to >= 0) & (to < n)
        send(lambda: remote(
            slab_of(src(chunk), i), slab_of(dg.at[chunk], i),
            d_send.at[slot, i], d_recv.at[chunk, i], {"col": to},
        ), ok)

    def owned(src, chunk, slot, i):
        for k in range(pieces):
            first = chunk * cols + k * width
            target = first // out_rows
            place = (first - target * out_rows) // width
            ok = (chunk >= 0) & (chunk < n)

            def ends(k=k, place=place):
                dst = dr_ref.at[
                    pl.ds(p * rows + i * slab, slab),
                    pl.ds(pl.multiple_of(place * width, width), width),
                ]
                return slab_of(src(chunk), i).at[:, pl.ds(k * width, width)], dst, a_recv.at[p, place]

            def make_remote(ends=ends, target=target, k=k):
                s, t, sem = ends()
                return remote(s, t, a_send.at[slot, i * pieces + k], sem, in_plane(target))

            def make_local(ends=ends):
                return pltpu.make_async_copy(*ends())

            send(make_remote, ok & (target != p))
            pl.when(ok & (target == p))(lambda m=make_local: m().start())

    for i in range(slabs):
        owned(lambda chunk: d_ref, c, 0, i)

    def received(chunk):
        return remote(
            xg.at[chunk], xg.at[chunk], x_send.at[0], x_recv.at[chunk], {"col": lax.rem(c + 1, n)}
        )

    def work(chunk, wait, first, forward):
        load = pltpu.make_async_copy(
            h_ref.at[pl.ds(pl.multiple_of(chunk * cols, cols), cols)], hbuf, h_sem
        )
        load.start()
        wait()
        forward()
        load.wait()

        @pl.loop(0, cols // tile)
        def _(j):
            at = pl.ds(pl.multiple_of(j * tile, tile), tile)
            term = jnp.dot(xg[chunk], hbuf[:, at], preferred_element_type=jnp.float32)
            y[:, at] = term if first else y[:, at] + term

    work(c, own_x.wait, True, lambda: None)
    for d in range(1, n):
        for side in (0, 1):
            direction = 1 - 2 * side
            chunk = c - direction * d
            ok = (chunk >= 0) & (chunk < n)
            to = c + direction
            slot = 2 * d + side

            def make(chunk=chunk, to=to, slot=slot):
                return remote(xg.at[chunk], xg.at[chunk], x_send.at[slot], x_recv.at[chunk], {"col": to})

            @pl.when(ok)
            def _():
                def forward():
                    if d < n - 1:
                        pl.when((to >= 0) & (to < n))(lambda: make().start())

                work(chunk, lambda: received(chunk).wait_recv(), False, forward)

            if d < n - 1:
                pending.append((make, ok & (to >= 0) & (to < n)))

    def own_slab(i):
        for side in (0, 1):
            pass_on(lambda chunk: d_ref, c, 1 - 2 * side, side, i)

    own_slab(0)

    pp[...] = jnp.zeros_like(pp)

    @pl.loop(0, cols // tile)
    def _(j):
        at = pl.ds(pl.multiple_of(j * tile, tile), tile)
        pp[...] += lax.dot_general(
            y[:, at].astype(jnp.bfloat16), xg[c, :, at],
            (((1,), (1,)), ((), ())), preferred_element_type=jnp.float32,
        )

    def rows_of(ref, index):
        return ref.at[pl.ds(pl.multiple_of(index * part, part), part)]

    for step in range(1, n):
        to = lax.rem(c + step, n)
        send(lambda step=step, to=to: remote(
            rows_of(pp, to), pin.at[c], p_send.at[step], p_recv.at[c], {"col": to}
        ))

    for i in range(1, min(2, slabs)):
        own_slab(i)

    def d_step(d, i):
        for side in (0, 1):
            direction = 1 - 2 * side
            chunk = c - direction * d
            ok = (chunk >= 0) & (chunk < n)

            def arrived(chunk=chunk):
                return remote(
                    slab_of(dg.at[chunk], i), slab_of(dg.at[chunk], i),
                    d_send.at[0, i], d_recv.at[chunk, i], {"col": lax.rem(c + 1, n)},
                )

            pl.when(ok)(lambda arrived=arrived: arrived().wait_recv())
            if d < n - 1:
                pass_on(lambda ch: dg.at[ch], chunk, direction, 2 * d + side, i)
            owned(lambda ch: dg.at[ch], chunk, 2 * d + side, i)

    def c_step():
        own_d.wait()
        for step in range(1, half):
            source = same_parity(-step)
            remote(
                d_ref, block(dc_ref, source), c_send.at[0], c_recv.at[source], in_plane(mate)
            ).wait_recv()
            send(lambda step=step, source=source: remote(
                block(dc_ref, source), block(dc_ref, source),
                c_send.at[half + step], c_recv.at[source], in_plane(mate),
            ))

    def sum_step():
        total = rows_of(pp, c)[...]
        for step in range(1, n):
            source = lax.rem(c - step + n, n)
            remote(
                rows_of(pp, source), pin.at[source], p_send.at[1], p_recv.at[source],
                {"col": source},
            ).wait_recv()
            total = total + pin[source]
        same = rows_of(segt_ref, c)[...] == seg_ref[...]
        krow[...] = jnp.where(same, total, jnp.float32(0.0)).astype(jnp.bfloat16)
        dst = rows_of(k_ref.at[p], c)
        own_k = pltpu.make_async_copy(krow, dst, local.at[2])
        own_k.start()
        for step in range(1, n):
            to = lax.rem(c + step, n)
            send(lambda step=step, to=to: remote(
                krow, rows_of(k_ref.at[p], c), kz_send.at[step], kz_recv.at[c], {"col": to}
            ))
        own_k.wait()

    def square_step():
        for step in range(1, n):
            source = lax.rem(c - step + n, n)
            remote(
                krow, rows_of(k_ref.at[p], source), kz_send.at[1], kz_recv.at[source],
                {"col": source},
            ).wait_recv()
        send(lambda: remote(k_ref.at[p], k_ref.at[p], k_send.at[0], k_recv.at[p], in_plane(mate)))
        for step in range(1, half):
            send(lambda step=step: remote(
                k_ref.at[p], k_ref.at[p], k_send.at[step], k_recv.at[p],
                in_plane(same_parity(step)),
            ))

    def square_relay():
        for step in range(1, half):
            source = same_parity(-step)
            remote(
                k_ref.at[p], k_ref.at[source], k_send.at[0], k_recv.at[source], in_plane(mate)
            ).wait_recv()
            send(lambda step=step, source=source: remote(
                k_ref.at[source], k_ref.at[source],
                k_send.at[half + step], k_recv.at[source], in_plane(mate),
            ))

    def z_step(source, arrive):
        if arrive:
            remote(
                d_ref, block(dc_ref, source), c_send.at[0], c_recv.at[source], in_plane(mate)
            ).wait_recv()
            remote(
                k_ref.at[p], k_ref.at[source], k_send.at[0], k_recv.at[source], in_plane(mate)
            ).wait_recv()
        loads = (
            pltpu.make_async_copy(block(dc_ref, source), dbuf, z_sem.at[0]),
            pltpu.make_async_copy(k_ref.at[source], kbuf, z_sem.at[1]),
        )
        for load in loads:
            load.start()
        for load in loads:
            load.wait()

        @pl.loop(0, cols // tile)
        def _(j):
            at = pl.ds(pl.multiple_of(j * tile, tile), tile)
            z = jnp.dot(kbuf[...], dbuf[:, at], preferred_element_type=jnp.float32)
            zbuf[:, at] = z.astype(jnp.bfloat16)

        store = pltpu.make_async_copy(zbuf, block(z_ref, source), z_sem.at[2])
        store.start()
        store.wait()

    c_step()
    stages = [sum_step, square_step, square_relay]
    for step in range(half):
        stages.append(lambda step=step: z_step(same_parity(step), False))
    for step in range(half):
        other = 2 * lax.rem(p // 2 + step, half) + 1 - parity
        stages.append(lambda other=other: z_step(other, True))
    for i in range(slabs):
        for d in range(1, n):
            if stages:
                stages.pop(0)()
            d_step(d, i)
            if d == 1 and i + 2 < slabs:
                own_slab(i + 2)
    for stage in stages:
        stage()

    for source in range(planes):
        for place in range(per_row_block):
            dst = dr_ref.at[pl.ds(source * rows, rows), pl.ds(place * width, width)]
            pltpu.make_async_copy(dst, dst, a_recv.at[source, place]).wait()
    for make, condition in pending:
        if condition is None:
            make().wait_send()
        else:
            pl.when(condition)(lambda make=make: make().wait_send())


def product_kernel(z_ref, dr_ref, out_ref, turned):
    tokens, out_rows = dr_ref.shape
    deep, high = min(tokens, 512), min(out_rows, 256)

    @pl.when(pl.program_id(0) == 0)
    def _():
        @pl.loop(0, tokens // deep)
        def _(j):
            at = pl.ds(pl.multiple_of(j * deep, deep), deep)
            turned[:, at] = dr_ref[at, :].T

    @pl.loop(0, out_rows // high)
    def _(j):
        at = pl.ds(pl.multiple_of(j * high, high), high)
        out_ref[at, :] = jnp.dot(turned[at, :], z_ref[...], preferred_element_type=jnp.float32)


def per_device(n, seqs, tps, inputs, grads, h_in, segments):
    rows, cols = inputs.shape
    planes = seqs * tps
    out_rows = n * cols // planes
    width = min(cols, out_rows)
    part = rows // n
    slabs = 4
    tokens, tile = planes * rows, min(cols, 256)
    dma = pltpu.SemaphoreType.DMA
    any_space = pl.BlockSpec(memory_space=pl.ANY)
    vmem = pl.BlockSpec(memory_space=pltpu.VMEM)
    owned_grads, _, _, products = pl.pallas_call(
        functools.partial(gather_kernel, n, tps, planes, out_rows, slabs),
        out_shape=(
            jax.ShapeDtypeStruct((planes * rows, out_rows), jnp.bfloat16),
            jax.ShapeDtypeStruct((planes * rows, cols), jnp.bfloat16),
            jax.ShapeDtypeStruct((planes, rows, rows), jnp.bfloat16),
            jax.ShapeDtypeStruct((tokens, cols), jnp.bfloat16),
        ),
        in_specs=[any_space, any_space, any_space, vmem, vmem],
        out_specs=(any_space,) * 4,
        scratch_shapes=[
            pltpu.VMEM((n, rows, cols), jnp.bfloat16),
            pltpu.VMEM((n, rows, cols), jnp.bfloat16),
            pltpu.VMEM((cols, cols), jnp.bfloat16),
            pltpu.VMEM((rows, cols), jnp.float32),
            pltpu.VMEM((rows, rows), jnp.float32),
            pltpu.VMEM((n, part, rows), jnp.float32),
            pltpu.VMEM((part, rows), jnp.bfloat16),
            pltpu.VMEM((rows, cols), jnp.bfloat16),
            pltpu.VMEM((rows, rows), jnp.bfloat16),
            pltpu.VMEM((rows, cols), jnp.bfloat16),
            dma((2 * n,)), dma((n,)),
            dma((2 * n, slabs)), dma((n, slabs)),
            dma((planes,)), dma((planes,)),
            dma((2 * n, slabs * (cols // width))), dma((planes, out_rows // width)),
            dma((n,)), dma((n,)),
            dma((n,)), dma((n,)),
            dma((planes,)), dma((planes,)),
            dma((3,)), dma, dma((3,)),
        ],
        compiler_params=pltpu.CompilerParams(
            collective_id=0, has_side_effects=True, vmem_limit_bytes=48 * MIB
        ),
    )(inputs, grads, h_in, segments, segments.reshape(rows, 1))
    return pl.pallas_call(
        product_kernel,
        grid=(cols // tile,),
        out_shape=jax.ShapeDtypeStruct((out_rows, cols), jnp.float32),
        in_specs=[
            pl.BlockSpec((tokens, tile), lambda j: (0, j)),
            pl.BlockSpec((tokens, out_rows), lambda j: (0, 0)),
        ],
        out_specs=pl.BlockSpec((out_rows, tile), lambda j: (0, j)),
        scratch_shapes=[pltpu.VMEM((out_rows, tokens), jnp.bfloat16)],
        compiler_params=pltpu.CompilerParams(vmem_limit_bytes=48 * MIB),
    )(products, owned_grads)


def solution(mesh):
    placed = (
        P(("seq", "tp"), "col"),
        P(("seq", "tp"), "col"),
        P(None, "col"),
        P(("seq", "tp"), None),
    )
    sizes = (mesh.shape["col"], mesh.shape["seq"], mesh.shape["tp"])
    return jax.shard_map(
        functools.partial(per_device, *sizes),
        mesh=mesh, in_specs=placed, out_specs=P(("seq", "tp"), "col"), check_vma=False,
    )
```

```python
import functools

import jax
import jax.numpy as jnp
from jax import lax
from jax.experimental import pallas as pl
from jax.experimental.pallas import tpu as pltpu
from jax.sharding import PartitionSpec as P

MESH = pl.DeviceIdType.MESH
MIB = 1 << 20


def gather_kernel(
    n, tps, planes, out_rows, slabs,
    x_ref, d_ref, h_ref, seg_ref, segt_ref,
    dr_ref, dc_ref, k_ref, z_ref, h2_ref,
    xg, dg, hbuf, y, pp, pin, krow, dbuf, kbuf, zbuf,
    x_send, x_recv, d_send, d_recv, c_send, c_recv, a_send, a_recv,
    p_send, p_recv, kz_send, kz_recv, k_send, k_recv, local, h_sem, z_sem,
    e_send, e_recv, f_send, f_recv,
):
    rows, cols = x_ref.shape
    width = min(cols, out_rows)
    pieces, per_row_block = cols // width, out_rows // width
    half = planes // 2
    part, slab = rows // n, rows // slabs
    tile = min(cols, 256)
    c = lax.axis_index("col")
    p = lax.axis_index("seq") * tps + lax.axis_index("tp")
    parity, mate = lax.rem(p, 2), p + 1 - 2 * lax.rem(p, 2)
    pending = []
    share = cols // planes
    is_edge = (c == 0) | (c == n - 1)
    is_inner = (c == 1) | (c == n - 2)
    inner = 1 + (c // (n - 1)) * (n - 3)
    edge = (n - 1) * (c // (n - 2))

    def in_plane(index):
        return {"seq": index // tps, "tp": lax.rem(index, tps)}

    def same_parity(step):
        return 2 * lax.rem(p // 2 + step + half, half) + parity

    def send(make, condition=None):
        if condition is None:
            make().start()
        else:
            pl.when(condition)(lambda: make().start())
        pending.append((make, condition))

    def remote(src, dst, ssem, rsem, to):
        return pltpu.make_async_remote_copy(
            src_ref=src, dst_ref=dst, send_sem=ssem, recv_sem=rsem,
            device_id=to, device_id_type=MESH,
        )

    barrier = pltpu.get_barrier_semaphore()
    for step in range(1, n):
        pl.semaphore_signal(
            barrier, inc=1, device_id={"col": lax.rem(c + step, n)}, device_id_type=MESH
        )
    for step in range(1, planes):
        pl.semaphore_signal(
            barrier, inc=1, device_id=in_plane(lax.rem(p + step, planes)), device_id_type=MESH
        )
    pl.semaphore_wait(barrier, n - 1 + planes - 1)

    for side in (0, 1):
        def make(side=side):
            return remote(x_ref, xg.at[c], x_send.at[side], x_recv.at[c], {"col": c + 1 - 2 * side})

        send(make, (c > 1) if side else (c + 2 < n))
    own_x = pltpu.make_async_copy(x_ref, xg.at[c], local.at[0])
    own_x.start()

    def h_share(ref, index, chunk=0):
        return ref.at[pl.ds(pl.multiple_of(chunk * cols + index * share, share), share)]

    send(lambda: remote(
        h_share(h_ref, p, inner), h_share(h2_ref, p), e_send, e_recv, {"col": inner}
    ), is_edge)

    def h_fan_out():
        @pl.when(is_inner)
        def _():
            remote(h_share(h2_ref, p), h_share(h2_ref, p), e_send, e_recv, {"col": edge}).wait_recv()

        send(lambda: remote(
            h_share(h2_ref, p), h_share(h2_ref, p), f_send.at[0], f_recv.at[p], in_plane(mate)
        ), is_inner)
        for step in range(1, half):
            send(lambda step=step: remote(
                h_share(h2_ref, p), h_share(h2_ref, p), f_send.at[step], f_recv.at[p],
                in_plane(same_parity(step)),
            ), is_inner)

    def h_arrived(source):
        remote(
            h_share(h2_ref, source), h_share(h2_ref, source), f_send.at[0], f_recv.at[source],
            in_plane(mate),
        ).wait_recv()

    def h_relay():
        for step in range(1, half):
            source = same_parity(-step)
            pl.when(is_inner)(lambda source=source: h_arrived(source))
            send(lambda step=step, source=source: remote(
                h_share(h2_ref, source), h_share(h2_ref, source),
                f_send.at[half + step], f_recv.at[source], in_plane(mate),
            ), is_inner)

    def block(ref, index):
        return ref.at[pl.ds(index * rows, rows)]

    own_d = pltpu.make_async_copy(d_ref, block(dc_ref, p), local.at[1])
    own_d.start()
    send(lambda: remote(d_ref, block(dc_ref, p), c_send.at[0], c_recv.at[p], in_plane(mate)))
    for step in range(1, half):
        send(lambda step=step: remote(
            d_ref, block(dc_ref, p), c_send.at[step], c_recv.at[p], in_plane(same_parity(step))
        ))

    def slab_of(ref, i):
        return ref.at[pl.ds(i * slab, slab)]

    def pass_on(src, chunk, direction, slot, i, also=True):
        to = c + direction
        ok = (chunk >= 0) & (chunk < n) & (to >= 0) & (to < n) & also
        send(lambda: remote(
            slab_of(src(chunk), i), slab_of(dg.at[chunk], i),
            d_send.at[slot, i], d_recv.at[chunk, i], {"col": to},
        ), ok)

    def owned(src, chunk, slot, i):
        for k in range(pieces):
            first = chunk * cols + k * width
            target = first // out_rows
            place = (first - target * out_rows) // width
            ok = (chunk >= 0) & (chunk < n)

            def ends(k=k, place=place):
                dst = dr_ref.at[
                    pl.ds(p * rows + i * slab, slab),
                    pl.ds(pl.multiple_of(place * width, width), width),
                ]
                return slab_of(src(chunk), i).at[:, pl.ds(k * width, width)], dst, a_recv.at[p, place]

            def make_remote(ends=ends, target=target, k=k):
                s, t, sem = ends()
                return remote(s, t, a_send.at[slot, i * pieces + k], sem, in_plane(target))

            def make_local(ends=ends):
                return pltpu.make_async_copy(*ends())

            send(make_remote, ok & (target != p))
            pl.when(ok & (target == p))(lambda m=make_local: m().start())

    for i in range(slabs):
        owned(lambda chunk: d_ref, c, 0, i)

    def received(chunk):
        return remote(
            xg.at[chunk], xg.at[chunk], x_send.at[0], x_recv.at[chunk], {"col": lax.rem(c + 1, n)}
        )

    def work(chunk, wait, first, forward):
        load = pltpu.make_async_copy(
            h_ref.at[pl.ds(pl.multiple_of(chunk * cols, cols), cols)], hbuf, h_sem
        )
        load.start()
        wait()
        forward()
        load.wait()

        @pl.loop(0, cols // tile)
        def _(j):
            at = pl.ds(pl.multiple_of(j * tile, tile), tile)
            term = jnp.dot(xg[chunk], hbuf[:, at], preferred_element_type=jnp.float32)
            y[:, at] = term if first else y[:, at] + term

    ahead = min(2, slabs)

    def own_slab(i, side, also=True):
        pass_on(lambda chunk: d_ref, c, 1 - 2 * side, side, i, also)

    def own_ahead(d):
        for side in (0, 1):
            for i in range(ahead):
                own_slab(i, side, (c == n - 1 - d) if side else (c == d))

    own_ahead(0)
    work(c, own_x.wait, True, lambda: None)
    for d in range(1, n):
        for side in (0, 1):
            direction = 1 - 2 * side
            chunk = c - direction * d
            ok = (chunk >= 0) & (chunk < n)
            if d == 1:
                ok = ok & jnp.logical_not(is_edge)
            to = c + direction
            slot = 2 * d + side

            def make(chunk=chunk, to=to, slot=slot):
                return remote(xg.at[chunk], xg.at[chunk], x_send.at[slot], x_recv.at[chunk], {"col": to})

            @pl.when(ok)
            def _():
                def forward():
                    if d < n - 1:
                        pl.when((to >= 0) & (to < n))(lambda: make().start())

                work(chunk, lambda: received(chunk).wait_recv(), False, forward)

            if d < n - 1:
                pending.append((make, ok & (to >= 0) & (to < n)))
        if d < n - 1:
            own_ahead(d)
        if d == 1:
            h_fan_out()
        if d == 2:
            h_relay()

    pp[...] = jnp.zeros_like(pp)

    def add_squares(chunk):
        @pl.loop(0, cols // tile)
        def _(j):
            at = pl.ds(pl.multiple_of(j * tile, tile), tile)
            pp[...] += lax.dot_general(
                y[:, at].astype(jnp.bfloat16), xg[chunk, :, at],
                (((1,), (1,)), ((), ())), preferred_element_type=jnp.float32,
            )

    add_squares(c)

    @pl.when(is_inner)
    def _():
        for step in range(half):
            h_arrived(2 * lax.rem(p // 2 + step, half) + 1 - parity)
        load = pltpu.make_async_copy(h2_ref, hbuf, h_sem)
        load.start()
        load.wait()

        @pl.loop(0, cols // tile)
        def _(j):
            at = pl.ds(pl.multiple_of(j * tile, tile), tile)
            y[:, at] = jnp.dot(xg[c], hbuf[:, at], preferred_element_type=jnp.float32)

        add_squares(edge)

    def rows_of(ref, index):
        return ref.at[pl.ds(pl.multiple_of(index * part, part), part)]

    for step in range(1, n):
        to = lax.rem(c + step, n)
        send(lambda step=step, to=to: remote(
            rows_of(pp, to), pin.at[c], p_send.at[step], p_recv.at[c], {"col": to}
        ))

    def d_step(d, i):
        for side in (0, 1):
            direction = 1 - 2 * side
            chunk = c - direction * d
            ok = (chunk >= 0) & (chunk < n)

            def arrived(chunk=chunk):
                return remote(
                    slab_of(dg.at[chunk], i), slab_of(dg.at[chunk], i),
                    d_send.at[0, i], d_recv.at[chunk, i], {"col": lax.rem(c + 1, n)},
                )

            pl.when(ok)(lambda arrived=arrived: arrived().wait_recv())
            if d < n - 1:
                pass_on(lambda ch: dg.at[ch], chunk, direction, 2 * d + side, i)
            owned(lambda ch: dg.at[ch], chunk, 2 * d + side, i)

    def c_step():
        own_d.wait()
        for step in range(1, half):
            source = same_parity(-step)
            remote(
                d_ref, block(dc_ref, source), c_send.at[0], c_recv.at[source], in_plane(mate)
            ).wait_recv()
            send(lambda step=step, source=source: remote(
                block(dc_ref, source), block(dc_ref, source),
                c_send.at[half + step], c_recv.at[source], in_plane(mate),
            ))

    def sum_step():
        total = rows_of(pp, c)[...]
        for step in range(1, n):
            source = lax.rem(c - step + n, n)
            remote(
                rows_of(pp, source), pin.at[source], p_send.at[1], p_recv.at[source],
                {"col": source},
            ).wait_recv()
            total = total + pin[source]
        same = rows_of(segt_ref, c)[...] == seg_ref[...]
        krow[...] = jnp.where(same, total, jnp.float32(0.0)).astype(jnp.bfloat16)
        dst = rows_of(k_ref.at[p], c)
        own_k = pltpu.make_async_copy(krow, dst, local.at[2])
        own_k.start()
        for step in range(1, n):
            to = lax.rem(c + step, n)
            send(lambda step=step, to=to: remote(
                krow, rows_of(k_ref.at[p], c), kz_send.at[step], kz_recv.at[c], {"col": to}
            ))
        own_k.wait()

    def square_step():
        for step in range(1, n):
            source = lax.rem(c - step + n, n)
            remote(
                krow, rows_of(k_ref.at[p], source), kz_send.at[1], kz_recv.at[source],
                {"col": source},
            ).wait_recv()
        send(lambda: remote(k_ref.at[p], k_ref.at[p], k_send.at[0], k_recv.at[p], in_plane(mate)))
        for step in range(1, half):
            send(lambda step=step: remote(
                k_ref.at[p], k_ref.at[p], k_send.at[step], k_recv.at[p],
                in_plane(same_parity(step)),
            ))

    def square_relay():
        for step in range(1, half):
            source = same_parity(-step)
            remote(
                k_ref.at[p], k_ref.at[source], k_send.at[0], k_recv.at[source], in_plane(mate)
            ).wait_recv()
            send(lambda step=step, source=source: remote(
                k_ref.at[source], k_ref.at[source],
                k_send.at[half + step], k_recv.at[source], in_plane(mate),
            ))

    def z_step(source, arrive):
        if arrive:
            remote(
                d_ref, block(dc_ref, source), c_send.at[0], c_recv.at[source], in_plane(mate)
            ).wait_recv()
            remote(
                k_ref.at[p], k_ref.at[source], k_send.at[0], k_recv.at[source], in_plane(mate)
            ).wait_recv()
        loads = (
            pltpu.make_async_copy(block(dc_ref, source), dbuf, z_sem.at[0]),
            pltpu.make_async_copy(k_ref.at[source], kbuf, z_sem.at[1]),
        )
        for load in loads:
            load.start()
        for load in loads:
            load.wait()

        @pl.loop(0, cols // tile)
        def _(j):
            at = pl.ds(pl.multiple_of(j * tile, tile), tile)
            z = jnp.dot(kbuf[...], dbuf[:, at], preferred_element_type=jnp.float32)
            zbuf[:, at] = z.astype(jnp.bfloat16)

        store = pltpu.make_async_copy(zbuf, block(z_ref, source), z_sem.at[2])
        store.start()
        store.wait()

    c_step()
    stages = [sum_step, square_step, square_relay]
    for step in range(half):
        stages.append(lambda step=step: z_step(same_parity(step), False))
    for step in range(half):
        other = 2 * lax.rem(p // 2 + step, half) + 1 - parity
        stages.append(lambda other=other: z_step(other, True))
    for i in range(slabs):
        for d in range(1, n):
            if stages:
                stages.pop(0)()
            d_step(d, i)
            if d == 1 and i + ahead < slabs:
                own_slab(i + ahead, 0)
                own_slab(i + ahead, 1)
    for stage in stages:
        stage()

    for source in range(planes):
        for place in range(per_row_block):
            dst = dr_ref.at[pl.ds(source * rows, rows), pl.ds(place * width, width)]
            pltpu.make_async_copy(dst, dst, a_recv.at[source, place]).wait()
    for make, condition in pending:
        if condition is None:
            make().wait_send()
        else:
            pl.when(condition)(lambda make=make: make().wait_send())


def product_kernel(z_ref, dr_ref, out_ref, turned):
    tokens, out_rows = dr_ref.shape
    deep, high = min(tokens, 512), min(out_rows, 256)

    @pl.when(pl.program_id(0) == 0)
    def _():
        @pl.loop(0, tokens // deep)
        def _(j):
            at = pl.ds(pl.multiple_of(j * deep, deep), deep)
            turned[:, at] = dr_ref[at, :].T

    @pl.loop(0, out_rows // high)
    def _(j):
        at = pl.ds(pl.multiple_of(j * high, high), high)
        out_ref[at, :] = jnp.dot(turned[at, :], z_ref[...], preferred_element_type=jnp.float32)


def per_device(n, seqs, tps, inputs, grads, h_in, segments):
    rows, cols = inputs.shape
    planes = seqs * tps
    out_rows = n * cols // planes
    width = min(cols, out_rows)
    part = rows // n
    slabs = 4
    tokens, tile = planes * rows, min(cols, 256)
    dma = pltpu.SemaphoreType.DMA
    any_space = pl.BlockSpec(memory_space=pl.ANY)
    vmem = pl.BlockSpec(memory_space=pltpu.VMEM)
    owned_grads, _, _, products, _ = pl.pallas_call(
        functools.partial(gather_kernel, n, tps, planes, out_rows, slabs),
        out_shape=(
            jax.ShapeDtypeStruct((planes * rows, out_rows), jnp.bfloat16),
            jax.ShapeDtypeStruct((planes * rows, cols), jnp.bfloat16),
            jax.ShapeDtypeStruct((planes, rows, rows), jnp.bfloat16),
            jax.ShapeDtypeStruct((tokens, cols), jnp.bfloat16),
            jax.ShapeDtypeStruct((cols, cols), jnp.bfloat16),
        ),
        in_specs=[any_space, any_space, any_space, vmem, vmem],
        out_specs=(any_space,) * 5,
        scratch_shapes=[
            pltpu.VMEM((n, rows, cols), jnp.bfloat16),
            pltpu.VMEM((n, rows, cols), jnp.bfloat16),
            pltpu.VMEM((cols, cols), jnp.bfloat16),
            pltpu.VMEM((rows, cols), jnp.float32),
            pltpu.VMEM((rows, rows), jnp.float32),
            pltpu.VMEM((n, part, rows), jnp.float32),
            pltpu.VMEM((part, rows), jnp.bfloat16),
            pltpu.VMEM((rows, cols), jnp.bfloat16),
            pltpu.VMEM((rows, rows), jnp.bfloat16),
            pltpu.VMEM((rows, cols), jnp.bfloat16),
            dma((2 * n,)), dma((n,)),
            dma((2 * n, slabs)), dma((n, slabs)),
            dma((planes,)), dma((planes,)),
            dma((2 * n, slabs * (cols // width))), dma((planes, out_rows // width)),
            dma((n,)), dma((n,)),
            dma((n,)), dma((n,)),
            dma((planes,)), dma((planes,)),
            dma((3,)), dma, dma((3,)),
            dma, dma, dma((planes,)), dma((planes,)),
        ],
        compiler_params=pltpu.CompilerParams(
            collective_id=0, has_side_effects=True, vmem_limit_bytes=48 * MIB
        ),
    )(inputs, grads, h_in, segments, segments.reshape(rows, 1))
    return pl.pallas_call(
        product_kernel,
        grid=(cols // tile,),
        out_shape=jax.ShapeDtypeStruct((out_rows, cols), jnp.float32),
        in_specs=[
            pl.BlockSpec((tokens, tile), lambda j: (0, j)),
            pl.BlockSpec((tokens, out_rows), lambda j: (0, 0)),
        ],
        out_specs=pl.BlockSpec((out_rows, tile), lambda j: (0, j)),
        scratch_shapes=[pltpu.VMEM((out_rows, tokens), jnp.bfloat16)],
        compiler_params=pltpu.CompilerParams(vmem_limit_bytes=48 * MIB),
    )(products, owned_grads)


def solution(mesh):
    placed = (
        P(("seq", "tp"), "col"),
        P(("seq", "tp"), "col"),
        P(None, "col"),
        P(("seq", "tp"), None),
    )
    sizes = (mesh.shape["col"], mesh.shape["seq"], mesh.shape["tp"])
    return jax.shard_map(
        functools.partial(per_device, *sizes),
        mesh=mesh, in_specs=placed, out_specs=P(("seq", "tp"), "col"), check_vma=False,
    )
```

```python
import functools

import jax
import jax.numpy as jnp
from jax import lax
from jax.experimental import pallas as pl
from jax.experimental.pallas import tpu as pltpu
from jax.sharding import PartitionSpec as P

MESH = pl.DeviceIdType.MESH
MIB = 1 << 20


def gather_kernel(
    n, tps, planes, out_rows, slabs,
    x_ref, d_ref, h_ref, seg_ref, segt_ref,
    dr_ref, dc_ref, k_ref, z_ref,
    xg, dg, hbuf, y, pp, pin, krow, dbuf, kbuf, zbuf,
    x_send, x_recv, d_send, d_recv, c_send, c_recv, a_send, a_recv,
    p_send, p_recv, kz_send, kz_recv, k_send, k_recv, local, h_sem, z_sem,
):
    rows, cols = x_ref.shape
    width = min(cols, out_rows)
    pieces, per_row_block = cols // width, out_rows // width
    half = planes // 2
    part, slab = rows // n, rows // slabs
    tile = min(cols, 256)
    c = lax.axis_index("col")
    p = lax.axis_index("seq") * tps + lax.axis_index("tp")
    parity, mate = lax.rem(p, 2), p + 1 - 2 * lax.rem(p, 2)
    pending = []

    def in_plane(index):
        return {"seq": index // tps, "tp": lax.rem(index, tps)}

    def same_parity(step):
        return 2 * lax.rem(p // 2 + step + half, half) + parity

    def send(make, condition=None):
        if condition is None:
            make().start()
        else:
            pl.when(condition)(lambda: make().start())
        pending.append((make, condition))

    def remote(src, dst, ssem, rsem, to):
        return pltpu.make_async_remote_copy(
            src_ref=src, dst_ref=dst, send_sem=ssem, recv_sem=rsem,
            device_id=to, device_id_type=MESH,
        )

    barrier = pltpu.get_barrier_semaphore()
    for step in range(1, n):
        pl.semaphore_signal(
            barrier, inc=1, device_id={"col": lax.rem(c + step, n)}, device_id_type=MESH
        )
    for step in range(1, planes):
        pl.semaphore_signal(
            barrier, inc=1, device_id=in_plane(lax.rem(p + step, planes)), device_id_type=MESH
        )
    pl.semaphore_wait(barrier, n - 1 + planes - 1)

    for side in (0, 1):
        def make(side=side):
            return remote(x_ref, xg.at[c], x_send.at[side], x_recv.at[c], {"col": c + 1 - 2 * side})

        send(make, (c > 0) if side else (c + 1 < n))
    own_x = pltpu.make_async_copy(x_ref, xg.at[c], local.at[0])
    own_x.start()

    def block(ref, index):
        return ref.at[pl.ds(index * rows, rows)]

    own_d = pltpu.make_async_copy(d_ref, block(dc_ref, p), local.at[1])
    own_d.start()
    send(lambda: remote(d_ref, block(dc_ref, p), c_send.at[0], c_recv.at[p], in_plane(mate)))
    for step in range(1, half):
        send(lambda step=step: remote(
            d_ref, block(dc_ref, p), c_send.at[step], c_recv.at[p], in_plane(same_parity(step))
        ))

    def slab_of(ref, i):
        return ref.at[pl.ds(i * slab, slab)]

    def pass_on(src, chunk, direction, slot, i, also=True):
        to = c + direction
        ok = (chunk >= 0) & (chunk < n) & (to >= 0) & (to < n) & also
        send(lambda: remote(
            slab_of(src(chunk), i), slab_of(dg.at[chunk], i),
            d_send.at[slot, i], d_recv.at[chunk, i], {"col": to},
        ), ok)

    def owned(src, chunk, slot, i):
        for k in range(pieces):
            first = chunk * cols + k * width
            target = first // out_rows
            place = (first - target * out_rows) // width
            ok = (chunk >= 0) & (chunk < n)

            def ends(k=k, place=place):
                dst = dr_ref.at[
                    pl.ds(p * rows + i * slab, slab),
                    pl.ds(pl.multiple_of(place * width, width), width),
                ]
                return slab_of(src(chunk), i).at[:, pl.ds(k * width, width)], dst, a_recv.at[p, place]

            def make_remote(ends=ends, target=target, k=k):
                s, t, sem = ends()
                return remote(s, t, a_send.at[slot, i * pieces + k], sem, in_plane(target))

            def make_local(ends=ends):
                return pltpu.make_async_copy(*ends())

            send(make_remote, ok & (target != p))
            pl.when(ok & (target == p))(lambda m=make_local: m().start())

    for i in range(slabs):
        owned(lambda chunk: d_ref, c, 0, i)

    def received(chunk):
        return remote(
            xg.at[chunk], xg.at[chunk], x_send.at[0], x_recv.at[chunk], {"col": lax.rem(c + 1, n)}
        )

    def work(chunk, wait, first, forward):
        load = pltpu.make_async_copy(
            h_ref.at[pl.ds(pl.multiple_of(chunk * cols, cols), cols)], hbuf, h_sem
        )
        load.start()
        wait()
        forward()
        load.wait()

        @pl.loop(0, cols // tile)
        def _(j):
            at = pl.ds(pl.multiple_of(j * tile, tile), tile)
            term = jnp.dot(xg[chunk], hbuf[:, at], preferred_element_type=jnp.float32)
            y[:, at] = term if first else y[:, at] + term

    ahead = min(2, slabs)

    def own_slab(i, side, also=True):
        pass_on(lambda chunk: d_ref, c, 1 - 2 * side, side, i, also)

    def own_ahead(d):
        for side in (0, 1):
            for i in range(ahead):
                own_slab(i, side, (c == n - 1 - d) if side else (c == d))

    own_ahead(0)
    work(c, own_x.wait, True, lambda: None)
    for d in range(1, n):
        for side in (0, 1):
            direction = 1 - 2 * side
            chunk = c - direction * d
            ok = (chunk >= 0) & (chunk < n)
            to = c + direction
            slot = 2 * d + side

            def make(chunk=chunk, to=to, slot=slot):
                return remote(xg.at[chunk], xg.at[chunk], x_send.at[slot], x_recv.at[chunk], {"col": to})

            @pl.when(ok)
            def _():
                def forward():
                    if d < n - 1:
                        pl.when((to >= 0) & (to < n))(lambda: make().start())

                work(chunk, lambda: received(chunk).wait_recv(), False, forward)

            if d < n - 1:
                pending.append((make, ok & (to >= 0) & (to < n)))
        if d < n - 1:
            own_ahead(d)

    pp[...] = jnp.zeros_like(pp)

    @pl.loop(0, cols // tile)
    def _(j):
        at = pl.ds(pl.multiple_of(j * tile, tile), tile)
        pp[...] += lax.dot_general(
            y[:, at].astype(jnp.bfloat16), xg[c, :, at],
            (((1,), (1,)), ((), ())), preferred_element_type=jnp.float32,
        )

    def rows_of(ref, index):
        return ref.at[pl.ds(pl.multiple_of(index * part, part), part)]

    for step in range(1, n):
        to = lax.rem(c + step, n)
        send(lambda step=step, to=to: remote(
            rows_of(pp, to), pin.at[c], p_send.at[step], p_recv.at[c], {"col": to}
        ))

    def d_step(d, i):
        for side in (0, 1):
            direction = 1 - 2 * side
            chunk = c - direction * d
            ok = (chunk >= 0) & (chunk < n)

            def arrived(chunk=chunk):
                return remote(
                    slab_of(dg.at[chunk], i), slab_of(dg.at[chunk], i),
                    d_send.at[0, i], d_recv.at[chunk, i], {"col": lax.rem(c + 1, n)},
                )

            pl.when(ok)(lambda arrived=arrived: arrived().wait_recv())
            if d < n - 1:
                pass_on(lambda ch: dg.at[ch], chunk, direction, 2 * d + side, i)
            owned(lambda ch: dg.at[ch], chunk, 2 * d + side, i)

    def c_step():
        own_d.wait()
        for step in range(1, half):
            source = same_parity(-step)
            remote(
                d_ref, block(dc_ref, source), c_send.at[0], c_recv.at[source], in_plane(mate)
            ).wait_recv()
            send(lambda step=step, source=source: remote(
                block(dc_ref, source), block(dc_ref, source),
                c_send.at[half + step], c_recv.at[source], in_plane(mate),
            ))

    def sum_step():
        total = rows_of(pp, c)[...]
        for step in range(1, n):
            source = lax.rem(c - step + n, n)
            remote(
                rows_of(pp, source), pin.at[source], p_send.at[1], p_recv.at[source],
                {"col": source},
            ).wait_recv()
            total = total + pin[source]
        same = rows_of(segt_ref, c)[...] == seg_ref[...]
        krow[...] = jnp.where(same, total, jnp.float32(0.0)).astype(jnp.bfloat16)
        dst = rows_of(k_ref.at[p], c)
        own_k = pltpu.make_async_copy(krow, dst, local.at[2])
        own_k.start()
        for step in range(1, n):
            to = lax.rem(c + step, n)
            send(lambda step=step, to=to: remote(
                krow, rows_of(k_ref.at[p], c), kz_send.at[step], kz_recv.at[c], {"col": to}
            ))
        own_k.wait()

    def square_step():
        for step in range(1, n):
            source = lax.rem(c - step + n, n)
            remote(
                krow, rows_of(k_ref.at[p], source), kz_send.at[1], kz_recv.at[source],
                {"col": source},
            ).wait_recv()
        send(lambda: remote(k_ref.at[p], k_ref.at[p], k_send.at[0], k_recv.at[p], in_plane(mate)))
        for step in range(1, half):
            send(lambda step=step: remote(
                k_ref.at[p], k_ref.at[p], k_send.at[step], k_recv.at[p],
                in_plane(same_parity(step)),
            ))

    def square_relay():
        for step in range(1, half):
            source = same_parity(-step)
            remote(
                k_ref.at[p], k_ref.at[source], k_send.at[0], k_recv.at[source], in_plane(mate)
            ).wait_recv()
            send(lambda step=step, source=source: remote(
                k_ref.at[source], k_ref.at[source],
                k_send.at[half + step], k_recv.at[source], in_plane(mate),
            ))

    def z_step(source, arrive):
        if arrive:
            remote(
                d_ref, block(dc_ref, source), c_send.at[0], c_recv.at[source], in_plane(mate)
            ).wait_recv()
            remote(
                k_ref.at[p], k_ref.at[source], k_send.at[0], k_recv.at[source], in_plane(mate)
            ).wait_recv()
        loads = (
            pltpu.make_async_copy(block(dc_ref, source), dbuf, z_sem.at[0]),
            pltpu.make_async_copy(k_ref.at[source], kbuf, z_sem.at[1]),
        )
        for load in loads:
            load.start()
        for load in loads:
            load.wait()

        @pl.loop(0, cols // tile)
        def _(j):
            at = pl.ds(pl.multiple_of(j * tile, tile), tile)
            z = jnp.dot(kbuf[...], dbuf[:, at], preferred_element_type=jnp.float32)
            zbuf[:, at] = z.astype(jnp.bfloat16)

        store = pltpu.make_async_copy(zbuf, block(z_ref, source), z_sem.at[2])
        store.start()
        store.wait()

    stages = [sum_step, square_step, c_step, square_relay]
    for step in range(half):
        stages.append(lambda step=step: z_step(same_parity(step), False))
    for step in range(half):
        other = 2 * lax.rem(p // 2 + step, half) + 1 - parity
        stages.append(lambda other=other: z_step(other, True))
    for i in range(slabs):
        for d in range(1, n):
            if stages:
                stages.pop(0)()
            d_step(d, i)
            if d == 1 and i + ahead < slabs:
                own_slab(i + ahead, 0)
                own_slab(i + ahead, 1)
    for stage in stages:
        stage()

    for source in range(planes):
        for place in range(per_row_block):
            dst = dr_ref.at[pl.ds(source * rows, rows), pl.ds(place * width, width)]
            pltpu.make_async_copy(dst, dst, a_recv.at[source, place]).wait()
    for make, condition in pending:
        if condition is None:
            make().wait_send()
        else:
            pl.when(condition)(lambda make=make: make().wait_send())


def product_kernel(z_ref, dr_ref, out_ref, turned):
    tokens, out_rows = dr_ref.shape
    deep, high = min(tokens, 512), min(out_rows, 256)

    @pl.when(pl.program_id(0) == 0)
    def _():
        @pl.loop(0, tokens // deep)
        def _(j):
            at = pl.ds(pl.multiple_of(j * deep, deep), deep)
            turned[:, at] = dr_ref[at, :].T

    @pl.loop(0, out_rows // high)
    def _(j):
        at = pl.ds(pl.multiple_of(j * high, high), high)
        out_ref[at, :] = jnp.dot(turned[at, :], z_ref[...], preferred_element_type=jnp.float32)


def per_device(n, seqs, tps, inputs, grads, h_in, segments):
    rows, cols = inputs.shape
    planes = seqs * tps
    out_rows = n * cols // planes
    width = min(cols, out_rows)
    part = rows // n
    slabs = 4
    tokens, tile = planes * rows, min(cols, 256)
    dma = pltpu.SemaphoreType.DMA
    any_space = pl.BlockSpec(memory_space=pl.ANY)
    vmem = pl.BlockSpec(memory_space=pltpu.VMEM)
    owned_grads, _, _, products = pl.pallas_call(
        functools.partial(gather_kernel, n, tps, planes, out_rows, slabs),
        out_shape=(
            jax.ShapeDtypeStruct((planes * rows, out_rows), jnp.bfloat16),
            jax.ShapeDtypeStruct((planes * rows, cols), jnp.bfloat16),
            jax.ShapeDtypeStruct((planes, rows, rows), jnp.bfloat16),
            jax.ShapeDtypeStruct((tokens, cols), jnp.bfloat16),
        ),
        in_specs=[any_space, any_space, any_space, vmem, vmem],
        out_specs=(any_space,) * 4,
        scratch_shapes=[
            pltpu.VMEM((n, rows, cols), jnp.bfloat16),
            pltpu.VMEM((n, rows, cols), jnp.bfloat16),
            pltpu.VMEM((cols, cols), jnp.bfloat16),
            pltpu.VMEM((rows, cols), jnp.float32),
            pltpu.VMEM((rows, rows), jnp.float32),
            pltpu.VMEM((n, part, rows), jnp.float32),
            pltpu.VMEM((part, rows), jnp.bfloat16),
            pltpu.VMEM((rows, cols), jnp.bfloat16),
            pltpu.VMEM((rows, rows), jnp.bfloat16),
            pltpu.VMEM((rows, cols), jnp.bfloat16),
            dma((2 * n,)), dma((n,)),
            dma((2 * n, slabs)), dma((n, slabs)),
            dma((planes,)), dma((planes,)),
            dma((2 * n, slabs * (cols // width))), dma((planes, out_rows // width)),
            dma((n,)), dma((n,)),
            dma((n,)), dma((n,)),
            dma((planes,)), dma((planes,)),
            dma((3,)), dma, dma((3,)),
        ],
        compiler_params=pltpu.CompilerParams(
            collective_id=0, has_side_effects=True, vmem_limit_bytes=48 * MIB
        ),
    )(inputs, grads, h_in, segments, segments.reshape(rows, 1))
    return pl.pallas_call(
        product_kernel,
        grid=(cols // tile,),
        out_shape=jax.ShapeDtypeStruct((out_rows, cols), jnp.float32),
        in_specs=[
            pl.BlockSpec((tokens, tile), lambda j: (0, j)),
            pl.BlockSpec((tokens, out_rows), lambda j: (0, 0)),
        ],
        out_specs=pl.BlockSpec((out_rows, tile), lambda j: (0, j)),
        scratch_shapes=[pltpu.VMEM((out_rows, tokens), jnp.bfloat16)],
        compiler_params=pltpu.CompilerParams(vmem_limit_bytes=48 * MIB),
    )(products, owned_grads)


def solution(mesh):
    placed = (
        P(("seq", "tp"), "col"),
        P(("seq", "tp"), "col"),
        P(None, "col"),
        P(("seq", "tp"), None),
    )
    sizes = (mesh.shape["col"], mesh.shape["seq"], mesh.shape["tp"])
    return jax.shard_map(
        functools.partial(per_device, *sizes),
        mesh=mesh, in_specs=placed, out_specs=P(("seq", "tp"), "col"), check_vma=False,
    )
```
